32 devices in a mesh: seq: 8 (over z, x), fsdp: 4 (over y, core).
Axes of the slice: x: 2, y: 2, z: 4, core: 2. Of those that a mesh axis runs over, the one named last changes fastest.
Arguments:
- projected: bfloat16 [64, 65536], P('seq'), may hold values from -70 to 70
- cached: bfloat16 [128, 320, 7168], P('seq', None, 'fsdp'), may hold values from -6 to 6
- stream: bfloat16 [64, 7168], P('seq'), may hold values from -700 to 700
- norm_gain: float32 [7168], replicated, may hold values from 0.5 to 2
- routes: int32 [64, 8], P('seq'), may hold values from 0 to 255, as said below
- route_gates: float32 [64, 8], P('seq'), may hold values from 0.2 to 1
- gate_weight: bfloat16 [7168, 16384], P('fsdp', 'seq'), may hold values from -0.0625 to 0.0625
- up_weight: bfloat16 [7168, 16384], P('fsdp', 'seq'), may hold values from -0.0625 to 0.0625
- down_weight: bfloat16 [16384, 7168], P('seq', 'fsdp'), may hold values from -0.125 to 0.125
Outputs:
- attention: bfloat16 [64, 16384], P('seq')
- routed: bfloat16 [64, 7168], P('seq', 'fsdp')
The draws below stay inside these ranges and needn't reach their ends.
Inputs may be any that keep to these rules, and one draw needn't show every extreme that they name: `routes`: each row names 8 different experts. Within the 8 rows of one device, at most 2 rows name any one expert below 8, and in every such block some expert below 8 is named by exactly 2 rows.
All inputs are finite; a program needn't handle non-finite values.
Results may differ from the reference program's by a relative error of at most 0.0071.
Values may be sent and summed in bfloat16 or wider, within the bound.
A program may use at most 192 MiB of HBM per device.

```python
import math
import jax
import jax.numpy as jnp
from jax import lax

D = 7168
HEADS = 128
QK_DIM = 192
V_DIM = 128
FF = 2048
EXPERTS = 256
TOPK = 8
WAVE_EXPERTS = 8
CAPACITY = 2
TOK_DEV = 8
PREFIX = 7168
SPAN = 64
N_SEQ = 8


def draw_projected(key, part):
    key = jax.random.fold_in(key, 11)
    subkeys = jax.random.split(key, 1)
    full_shape = (SPAN, HEADS, 2 * QK_DIM + V_DIM)
    base_draw = jax.random.truncated_normal(subkeys[0], -6.0, 6.0, full_shape, jnp.float32)
    return base_draw.reshape(SPAN, HEADS * (2 * QK_DIM + V_DIM)).astype(jnp.bfloat16)


def draw_stream(key, part):
    key = jax.random.fold_in(key, 23)
    subkeys = jax.random.split(key, 3)
    full_shape = (SPAN, D)
    col_scale = jnp.exp(jax.random.uniform(subkeys[2], (1, D), jnp.float32, 0.0, math.log(10.0)))
    base_draw = jax.random.truncated_normal(subkeys[0], -6.0, 6.0, full_shape, jnp.float32)
    row_scale = jnp.exp(jax.random.uniform(subkeys[1], (SPAN, 1), jnp.float32, 0.0, math.log(10.0)))
    return (base_draw * row_scale * col_scale).astype(jnp.bfloat16)


def draw_routes(key, part):
    key = jax.random.fold_in(key, 37)
    subkeys = jax.random.split(key, 5)
    blocks = SPAN // TOK_DEV
    counts = jax.random.randint(subkeys[0], (blocks, WAVE_EXPERTS), 0, CAPACITY + 1)
    hot_expert = jax.random.randint(subkeys[1], (), 0, WAVE_EXPERTS)
    counts = jnp.where(jnp.arange(WAVE_EXPERTS)[None, :] == hot_expert, CAPACITY, counts)
    order_keys = jax.random.split(subkeys[2], blocks * WAVE_EXPERTS)
    orders = jax.vmap(lambda subkey: jax.random.permutation(subkey, TOK_DEV))(order_keys)
    orders = orders.reshape(blocks, WAVE_EXPERTS, TOK_DEV)
    positions = jnp.argsort(orders, axis=-1)
    taken_rows = positions < counts[:, :, None]
    taken_rows = jnp.transpose(taken_rows, (0, 2, 1))
    taken_rows = jnp.pad(taken_rows, ((0, 0), (0, 0), (0, TOPK - WAVE_EXPERTS)))
    spread = (EXPERTS - WAVE_EXPERTS) // TOPK
    other_ids = jax.random.randint(subkeys[3], (blocks, TOK_DEV, TOPK), 0, spread)
    slot_ids = jnp.arange(TOPK, dtype=jnp.int32)
    fallback = WAVE_EXPERTS + slot_ids[None, None, :] * spread + other_ids
    expert_ids = jnp.where(taken_rows, slot_ids[None, None, :], fallback)
    scores = jax.random.randint(subkeys[4], (blocks, TOK_DEV, TOPK), 0, 1 << 20) * TOPK + slot_ids[None, None, :]
    shuffle = jnp.argsort(scores, axis=-1)
    expert_ids = jnp.take_along_axis(expert_ids, shuffle, axis=-1)
    return expert_ids.reshape(SPAN, TOPK).astype(jnp.int32)


def level_of(own_key, dims, cuts, least, top_value):
    gain, own = 1.0, jax.random.fold_in(own_key, 6)
    for position, blocks in cuts:
        heights = jnp.exp(jax.random.uniform(jax.random.fold_in(own, position), (blocks,), jnp.float32, least / len(cuts), top_value / len(cuts)))
        gain = gain * jnp.repeat(heights, dims[position] // blocks).reshape([-1 if axis == position else 1 for axis in range(len(dims))])
    return gain


def centred(own_key, shape, deviation, reach, shards=(), held_as=jnp.bfloat16):
    result = jax.random.normal(own_key, shape, jnp.float32) * deviation
    if len(shards) > 0:
        result = level_of(own_key, shape, shards, -0.22, 0.18) * result
    return jnp.clip(result, min=-reach, max=reach).astype(held_as)


def setup_inputs(seed: int = 0) -> dict:
    streams_of = jax.random.split(jax.random.key(seed), 10)
    projected = draw_projected(jax.random.fold_in(streams_of[9], 71), 0)
    cached = centred(streams_of[1], (HEADS, QK_DIM + V_DIM, PREFIX), 1.0, 6.0, ((0, 8), (2, 4)))
    stream = draw_stream(jax.random.fold_in(streams_of[9], 71), 0)
    norm_gain = jnp.clip(jnp.exp(jax.random.uniform(streams_of[3], (D,), jnp.float32, math.log(0.5), math.log(2.0))), 0.5, 2.0)
    routes = draw_routes(jax.random.fold_in(streams_of[9], 71), 0)
    route_gates = jnp.clip(0.2 + 0.8 * jax.random.uniform(streams_of[5], (SPAN, TOPK), jnp.float32) ** level_of(streams_of[5], (SPAN, TOPK), ((0, 8),), -0.2, 0.2), 0.2, 1.0)
    gate_weight = centred(streams_of[6], (D, WAVE_EXPERTS * FF), D ** -0.5, 0.0625, ((0, 4), (1, 8)))
    up_weight = centred(streams_of[7], (D, WAVE_EXPERTS * FF), D ** -0.5, 0.0625, ((0, 4), (1, 8)))
    down_weight = centred(streams_of[8], (WAVE_EXPERTS * FF, D), FF ** -0.5, 0.125, ((0, 8), (1, 4)))
    return dict(projected=projected, cached=cached, stream=stream, norm_gain=norm_gain, routes=routes, route_gates=route_gates, gate_weight=gate_weight, up_weight=up_weight, down_weight=down_weight)


def score_block(queries, key_rows, value_rows, cache_keys, cache_values):
    score_scale = 1.0 / math.sqrt(queries.shape[1])
    contract = (((1,), (1,)), ((), ()))
    span_scores = lax.dot_general(queries, key_rows, contract, preferred_element_type=jnp.float32) * score_scale
    cache_scores = jnp.dot(queries, cache_keys, preferred_element_type=jnp.float32) * score_scale
    query_pos = jnp.arange(queries.shape[0], dtype=jnp.int32)
    key_pos = jnp.arange(key_rows.shape[0], dtype=jnp.int32)
    span_open = key_pos[None, :] <= query_pos[:, None]
    span_scores = jnp.where(span_open, span_scores, -jnp.inf)
    highest = jnp.maximum(lax.optimization_barrier(jnp.max(span_scores, axis=1)), lax.optimization_barrier(jnp.max(cache_scores, axis=1)))
    span_weights = jnp.where(span_open, jnp.exp(span_scores - highest[:, None]), 0.0)
    cache_weights = jnp.exp(cache_scores - highest[:, None])
    running = lax.optimization_barrier(jnp.sum(span_weights, axis=1)) + lax.optimization_barrier(jnp.sum(cache_weights, axis=1))
    weighted_sum = jnp.dot(span_weights.astype(jnp.bfloat16), value_rows, preferred_element_type=jnp.float32)
    weighted_sum = weighted_sum + lax.dot_general(cache_weights.astype(jnp.bfloat16), cache_values, contract, preferred_element_type=jnp.float32)
    return (weighted_sum / running[:, None]).astype(jnp.bfloat16)

def reference(projected, cached, stream, norm_gain, routes, route_gates, gate_weight, up_weight, down_weight):
    pack_width = 2 * QK_DIM + V_DIM
    heads_major = jnp.transpose(projected.reshape(SPAN, HEADS, pack_width), (1, 0, 2))

    def one_head(head_pair):
        stacked, stored = head_pair
        return score_block(stacked[:, :QK_DIM], stacked[:, QK_DIM:2 * QK_DIM], stacked[:, 2 * QK_DIM:], stored[:QK_DIM], stored[QK_DIM:])
    outputs = lax.map(one_head, (heads_major, cached))
    attention = jnp.transpose(outputs, (1, 0, 2)).reshape(SPAN, HEADS * V_DIM)
    group_size = N_SEQ // WAVE_EXPERTS
    slice_width = FF // group_size
    flat_rows = stream.astype(jnp.float32)
    normed = (flat_rows * lax.rsqrt(lax.optimization_barrier(jnp.mean(flat_rows * flat_rows, axis=1, keepdims=True)) + 1e-06) * norm_gain).astype(jnp.bfloat16)
    slot_total = SPAN // TOK_DEV * CAPACITY
    routed = jnp.zeros((SPAN, D), jnp.float32)
    for expert in range(WAVE_EXPERTS):
        matches = routes == expert
        weight = lax.optimization_barrier(jnp.sum(jnp.where(matches, route_gates, 0.0), axis=1))
        named_rows = jnp.any(matches, axis=1)
        named_count = jnp.sum(named_rows.astype(jnp.int32))
        picked = jnp.nonzero(named_rows, size=slot_total, fill_value=0)[0].astype(jnp.int32)
        valid_rows = jnp.arange(slot_total, dtype=jnp.int32) < named_count
        inputs = normed[picked]
        columns = slice(expert * FF, (expert + 1) * FF)
        gate_act = jnp.dot(inputs, gate_weight[:, columns], preferred_element_type=jnp.float32)
        upward = jnp.dot(inputs, up_weight[:, columns], preferred_element_type=jnp.float32)
        hidden = (jax.nn.silu(gate_act) * upward).astype(jnp.bfloat16)
        expert_down = down_weight[columns]

        def add_slice(slot_index, running):
            first_col = (slot_index * slice_width).astype(jnp.int32)
            hidden_piece = lax.dynamic_slice_in_dim(hidden, first_col, slice_width, 1)
            rows_down = lax.dynamic_slice_in_dim(expert_down, first_col, slice_width, 0)
            partial_value = jnp.dot(hidden_piece, rows_down, preferred_element_type=jnp.float32).astype(jnp.bfloat16)
            partial_value = lax.optimization_barrier(partial_value)
            return running + partial_value.astype(jnp.float32)
        output = lax.fori_loop(0, group_size, add_slice, jnp.zeros((slot_total, D), jnp.float32))
        contribution = jnp.where(valid_rows[:, None], weight[picked][:, None] * output, 0.0)
        routed = routed.at[picked].add(contribution)
    return (attention, routed.astype(jnp.bfloat16))
```

```python
import math

import jax
import jax.numpy as jnp
from jax import lax
from jax.sharding import PartitionSpec as P

QK_DIM = 192
V_DIM = 128
WAVE_EXPERTS = 8
CAPACITY = 2


def on_device(
    projected, cached, stream, norm_gain, routes, route_gates, gate_weight, up_weight, down_weight
):
    pack_width = 2 * QK_DIM + V_DIM
    heads_here = cached.shape[0]
    cache_len = cached.shape[2]
    gathered = lax.all_to_all(projected, "seq", split_axis=1, concat_axis=0, tiled=True)
    span_len = gathered.shape[0]
    heads_major = jnp.transpose(gathered.reshape(span_len, heads_here, pack_width), (1, 0, 2))
    quarter = span_len // lax.axis_size("fsdp")
    first_key = lax.axis_index("fsdp") * quarter
    rows_block = math.gcd(512, span_len)
    block_count = span_len // rows_block
    score_scale = 1.0 / math.sqrt(QK_DIM)
    contract = (((1,), (1,)), ((), ()))

    def head_scores(head_pair):
        stacked, stored = head_pair
        key_rows = lax.dynamic_slice_in_dim(stacked[:, QK_DIM : 2 * QK_DIM], first_key, quarter, 0)
        query_blocks = stacked[:, :QK_DIM].reshape(block_count, rows_block, QK_DIM)

        def one_block(queries):
            span_scores = (
                lax.dot_general(queries, key_rows, contract, preferred_element_type=jnp.float32)
                * score_scale
            )
            cache_scores = (
                jnp.dot(queries, stored[:QK_DIM], preferred_element_type=jnp.float32) * score_scale
            )
            return jnp.concatenate([span_scores, cache_scores], axis=1)

        return lax.map(one_block, query_blocks).reshape(span_len, quarter + cache_len)

    scores = lax.map(head_scores, (heads_major, cached))
    query_pos = jnp.arange(span_len, dtype=jnp.int32)
    key_pos = first_key + jnp.arange(quarter, dtype=jnp.int32)
    span_open = key_pos[None, :] <= query_pos[:, None]
    open_mask = jnp.concatenate([span_open, jnp.ones((span_len, cache_len), bool)], axis=1)
    scores = jnp.where(open_mask[None], scores, -jnp.inf)
    highest = lax.pmax(jnp.max(scores, axis=2), "fsdp")
    exp_weights = jnp.where(open_mask[None], jnp.exp(scores - highest[:, :, None]), 0.0)
    key_total = jnp.sum(exp_weights, axis=2)
    weights_bf = exp_weights.astype(jnp.bfloat16)

    def head_values(head_item):
        weights_row, stacked, stored = head_item
        value_rows = lax.dynamic_slice_in_dim(stacked[:, 2 * QK_DIM :], first_key, quarter, 0)
        span_part = jnp.dot(
            weights_row[:, :quarter], value_rows, preferred_element_type=jnp.float32
        )
        cache_part = lax.dot_general(
            weights_row[:, quarter:], stored[QK_DIM:], contract, preferred_element_type=jnp.float32
        )
        return span_part + cache_part

    weighted = lax.map(head_values, (weights_bf, heads_major, cached))
    weighted, key_total = lax.psum((weighted, key_total), "fsdp")
    outputs = (weighted / key_total[:, :, None]).astype(jnp.bfloat16)
    merged = jnp.transpose(outputs, (1, 0, 2)).reshape(span_len, heads_here * V_DIM)
    attention = lax.all_to_all(merged, "seq", split_axis=0, concat_axis=1, tiled=True)
    tokens = stream.astype(jnp.float32)
    tok_count = tokens.shape[0]
    slice_cols = gate_weight.shape[0]
    normed = (
        tokens * lax.rsqrt(jnp.mean(tokens * tokens, axis=1, keepdims=True) + 1e-06) * norm_gain
    ).astype(jnp.bfloat16)
    experts_here = jnp.arange(WAVE_EXPERTS, dtype=jnp.int32)
    matches = routes[:, :, None] == experts_here[None, None, :]
    hit_counts = jnp.sum(matches.astype(jnp.int32), axis=1)
    weight_of = jnp.sum(jnp.where(matches, route_gates[:, :, None], 0.0), axis=1)
    rank_rows = jnp.cumsum(hit_counts, axis=0) - 1
    slot_ids = jnp.arange(CAPACITY, dtype=jnp.int32)
    placed = (hit_counts[None, :, :] == 1) & (rank_rows[None, :, :] == slot_ids[:, None, None])
    placed = jnp.transpose(placed, (2, 0, 1)).astype(jnp.float32)
    slot_weight = jnp.einsum("ect,te->ec", placed, weight_of, precision=lax.Precision.HIGHEST)
    placed_flat = placed.reshape(WAVE_EXPERTS * CAPACITY, tok_count)
    send_rows = jnp.dot(
        placed_flat.astype(jnp.bfloat16), normed, preferred_element_type=jnp.float32
    ).astype(jnp.bfloat16)
    group_size = lax.axis_size("seq") // WAVE_EXPERTS
    send_rows = lax.dynamic_slice_in_dim(
        send_rows, lax.axis_index("fsdp") * slice_cols, slice_cols, 1
    )
    outgoing = jnp.broadcast_to(
        send_rows.reshape(WAVE_EXPERTS, 1, CAPACITY, slice_cols),
        (WAVE_EXPERTS, group_size, CAPACITY, slice_cols),
    )
    outgoing = outgoing.reshape(WAVE_EXPERTS * group_size, CAPACITY, slice_cols)
    received = lax.all_to_all(outgoing, "seq", split_axis=0, concat_axis=0, tiled=True)
    rows_in = received.reshape(-1, received.shape[2])
    gate_act = jnp.dot(rows_in, gate_weight, preferred_element_type=jnp.float32)
    upward = jnp.dot(rows_in, up_weight, preferred_element_type=jnp.float32)
    gate_act, upward = lax.psum((gate_act, upward), "fsdp")
    hidden = (jax.nn.silu(gate_act) * upward).astype(jnp.bfloat16)
    partial_value = jnp.dot(hidden, down_weight, preferred_element_type=jnp.float32).astype(
        jnp.bfloat16
    )
    partial_value = partial_value.reshape(received.shape[0], received.shape[1], slice_cols)
    result = lax.all_to_all(partial_value, "seq", split_axis=0, concat_axis=0, tiled=True)
    expert_out = jnp.sum(
        result.reshape(WAVE_EXPERTS, group_size, CAPACITY, slice_cols).astype(jnp.float32), axis=1
    )
    weighted_out = expert_out * slot_weight[:, :, None]
    mixed_rows = lax.dot_general(
        placed_flat,
        weighted_out.reshape(WAVE_EXPERTS * CAPACITY, slice_cols),
        (((0,), (0,)), ((), ())),
        precision=lax.Precision.HIGHEST,
    )
    routed = mixed_rows.astype(jnp.bfloat16)
    return (attention, routed)


def solution(mesh):
    placed = (
        P("seq", None),
        P("seq", None, "fsdp"),
        P("seq", None),
        P(),
        P("seq", None),
        P("seq", None),
        P("fsdp", "seq"),
        P("fsdp", "seq"),
        P("seq", "fsdp"),
    )
    return jax.shard_map(
        on_device,
        mesh=mesh,
        in_specs=placed,
        out_specs=(P("seq", None), P("seq", "fsdp")),
        check_vma=False,
    )
```

```python
import functools
import math

import jax
import jax.numpy as jnp
from jax import lax
from jax.experimental import pallas as pl
from jax.experimental.pallas import tpu as pltpu
from jax.sharding import PartitionSpec as P

QK_DIM = 192
V_DIM = 128
WAVE_EXPERTS = 8
CAPACITY = 2


def on_device(
    projected, cached, stream, norm_gain, routes, route_gates, gate_weight, up_weight, down_weight
):
    pack_width = 2 * QK_DIM + V_DIM
    heads_here = cached.shape[0]
    cache_len = cached.shape[2]
    gathered = lax.all_to_all(projected, "seq", split_axis=1, concat_axis=0, tiled=True)
    span_len = gathered.shape[0]
    heads_major = jnp.transpose(gathered.reshape(span_len, heads_here, pack_width), (1, 0, 2))
    quarter = span_len // lax.axis_size("fsdp")
    first_key = lax.axis_index("fsdp") * quarter
    rows_block = math.gcd(512, span_len)
    block_count = span_len // rows_block
    score_scale = 1.0 / math.sqrt(QK_DIM)
    contract = (((1,), (1,)), ((), ()))

    def head_scores(head_pair):
        stacked, stored = head_pair
        key_rows = lax.dynamic_slice_in_dim(stacked[:, QK_DIM : 2 * QK_DIM], first_key, quarter, 0)
        query_blocks = stacked[:, :QK_DIM].reshape(block_count, rows_block, QK_DIM)

        def one_block(queries):
            span_scores = (
                lax.dot_general(queries, key_rows, contract, preferred_element_type=jnp.float32)
                * score_scale
            )
            cache_scores = (
                jnp.dot(queries, stored[:QK_DIM], preferred_element_type=jnp.float32) * score_scale
            )
            return jnp.concatenate([span_scores, cache_scores], axis=1)

        return lax.map(one_block, query_blocks).reshape(span_len, quarter + cache_len)

    scores = lax.map(head_scores, (heads_major, cached))
    query_pos = jnp.arange(span_len, dtype=jnp.int32)
    key_pos = first_key + jnp.arange(quarter, dtype=jnp.int32)
    span_open = key_pos[None, :] <= query_pos[:, None]
    open_mask = jnp.concatenate([span_open, jnp.ones((span_len, cache_len), bool)], axis=1)
    scores = jnp.where(open_mask[None], scores, -jnp.inf)
    highest = lax.pmax(jnp.max(scores, axis=2), "fsdp")
    exp_weights = jnp.where(open_mask[None], jnp.exp(scores - highest[:, :, None]), 0.0)
    key_total = jnp.sum(exp_weights, axis=2)
    weights_bf = exp_weights.astype(jnp.bfloat16)

    def head_values(head_item):
        weights_row, stacked, stored = head_item
        value_rows = lax.dynamic_slice_in_dim(stacked[:, 2 * QK_DIM :], first_key, quarter, 0)
        span_part = jnp.dot(
            weights_row[:, :quarter], value_rows, preferred_element_type=jnp.float32
        )
        cache_part = lax.dot_general(
            weights_row[:, quarter:], stored[QK_DIM:], contract, preferred_element_type=jnp.float32
        )
        return span_part + cache_part

    weighted = lax.map(head_values, (weights_bf, heads_major, cached))
    weighted, key_total = lax.psum((weighted, key_total), "fsdp")
    outputs = (weighted / key_total[:, :, None]).astype(jnp.bfloat16)
    merged = jnp.transpose(outputs, (1, 0, 2)).reshape(span_len, heads_here * V_DIM)
    attention = lax.all_to_all(merged, "seq", split_axis=0, concat_axis=1, tiled=True)
    tokens = stream.astype(jnp.float32)
    tok_count = tokens.shape[0]
    slice_cols = gate_weight.shape[0]
    normed = (
        tokens * lax.rsqrt(jnp.mean(tokens * tokens, axis=1, keepdims=True) + 1e-06) * norm_gain
    ).astype(jnp.bfloat16)
    experts_here = jnp.arange(WAVE_EXPERTS, dtype=jnp.int32)
    matches = routes[:, :, None] == experts_here[None, None, :]
    hit_counts = jnp.sum(matches.astype(jnp.int32), axis=1)
    weight_of = jnp.sum(jnp.where(matches, route_gates[:, :, None], 0.0), axis=1)
    rank_rows = jnp.cumsum(hit_counts, axis=0) - 1
    slot_ids = jnp.arange(CAPACITY, dtype=jnp.int32)
    placed = (hit_counts[None, :, :] == 1) & (rank_rows[None, :, :] == slot_ids[:, None, None])
    placed = jnp.transpose(placed, (2, 0, 1)).astype(jnp.float32)
    slot_weight = jnp.einsum("ect,te->ec", placed, weight_of, precision=lax.Precision.HIGHEST)
    placed_flat = placed.reshape(WAVE_EXPERTS * CAPACITY, tok_count)
    send_rows = jnp.dot(
        placed_flat.astype(jnp.bfloat16), normed, preferred_element_type=jnp.float32
    ).astype(jnp.bfloat16)
    group_size = lax.axis_size("seq") // WAVE_EXPERTS
    send_rows = lax.dynamic_slice_in_dim(
        send_rows, lax.axis_index("fsdp") * slice_cols, slice_cols, 1
    )
    outgoing = jnp.broadcast_to(
        send_rows.reshape(WAVE_EXPERTS, 1, CAPACITY, slice_cols),
        (WAVE_EXPERTS, group_size, CAPACITY, slice_cols),
    )
    outgoing = outgoing.reshape(WAVE_EXPERTS * group_size, CAPACITY, slice_cols)
    received = lax.all_to_all(outgoing, "seq", split_axis=0, concat_axis=0, tiled=True)
    rows_in = received.reshape(-1, received.shape[2])
    gate_act = jnp.dot(rows_in, gate_weight, preferred_element_type=jnp.float32)
    upward = jnp.dot(rows_in, up_weight, preferred_element_type=jnp.float32)
    gate_act, upward = lax.psum((gate_act, upward), "fsdp")
    hidden = (jax.nn.silu(gate_act) * upward).astype(jnp.bfloat16)
    partial_value = jnp.dot(hidden, down_weight, preferred_element_type=jnp.float32).astype(
        jnp.bfloat16
    )
    partial_value = partial_value.reshape(received.shape[0], received.shape[1], slice_cols)
    result = lax.all_to_all(partial_value, "seq", split_axis=0, concat_axis=0, tiled=True)
    expert_out = jnp.sum(
        result.reshape(WAVE_EXPERTS, group_size, CAPACITY, slice_cols).astype(jnp.float32), axis=1
    )
    weighted_out = expert_out * slot_weight[:, :, None]
    mixed_rows = lax.dot_general(
        placed_flat,
        weighted_out.reshape(WAVE_EXPERTS * CAPACITY, slice_cols),
        (((0,), (0,)), ((), ())),
        precision=lax.Precision.HIGHEST,
    )
    routed = mixed_rows.astype(jnp.bfloat16)
    return (attention, routed)


MESH = pl.DeviceIdType.MESH
GROUP = 4
LOG2E = 1.4426950408889634


def one_kernel(
    n_seq,
    proj, cached, stream, gain, routes, gates, gate_w, up_w, down_w,
    att_out, routed_out,
    gath, q_buf, k_span, v_span, cache_v, gate_v, up_v, down_v,
    rows_out, rows_in, part, part_in, hid, down_out, down_in,
    o_own, o_buf, o_in, st_buf, st_in, fin, hop,
    load_sem, own_sem,
    rows_s, rows_r, proj_s, proj_r, q_s, q_r, part_s, part_r, hid_s, hid_r,
    dn_s, dn_r, o_s, o_r, st_s, st_r, fin_s, fin_r, hop_s, hop_r,
):
    f32, bf16 = jnp.float32, jnp.bfloat16
    s = lax.axis_index("seq")
    f = lax.axis_index("fsdp")
    f1 = f + 1 - 2 * lax.rem(f, 2)
    f2 = lax.rem(f + 2, 4)
    f3 = lax.rem(f1 + 2, 4)
    peers = (f, f1, f2, f3)
    width = stream.shape[1]
    cols = down_w.shape[1]
    heads = cached.shape[0] // GROUP
    pack = 2 * QK_DIM + V_DIM
    chunk_cols = heads * pack
    quarter = gate_w.shape[1] // GROUP
    toks = stream.shape[0]
    span = n_seq * toks
    scale2 = LOG2E / math.sqrt(QK_DIM)

    def remote(src, dst, ssem, rsem, seq_id, fs_id):
        return pltpu.make_async_remote_copy(
            src_ref=src, dst_ref=dst, send_sem=ssem, recv_sem=rsem,
            device_id=(seq_id, fs_id), device_id_type=MESH,
        )

    own_proj = pltpu.make_async_copy(
        proj.at[:, pl.ds(pl.multiple_of((s * GROUP + f) * chunk_cols, 128), chunk_cols)],
        gath.at[s], own_sem,
    )
    own_proj.start()
    loads = [
        pltpu.make_async_copy(gate_w, gate_v, load_sem.at[0]),
        pltpu.make_async_copy(up_w, up_v, load_sem.at[1]),
        pltpu.make_async_copy(down_w, down_v, load_sem.at[2]),
    ]
    cache_loads = []
    for x in range(GROUP):
        piece = pl.ds(peers[x] * heads, heads)
        cache_loads.append(
            pltpu.make_async_copy(cached.at[piece], cache_v.at[piece], load_sem.at[3 + x])
        )
    for copy in (loads[0], loads[1], cache_loads[0], cache_loads[1], loads[2],
                 cache_loads[2], cache_loads[3]):
        copy.start()

    barrier = pltpu.get_barrier_semaphore()
    for k in range(1, n_seq):
        pl.semaphore_signal(
            barrier, inc=1, device_id=(lax.rem(s + k, n_seq), f), device_id_type=MESH
        )
    for x in range(1, GROUP):
        pl.semaphore_signal(barrier, inc=1, device_id=(s, peers[x]), device_id_type=MESH)

    tokens = stream[...].astype(f32)
    inv = lax.rsqrt(jnp.sum(tokens * tokens, axis=1, keepdims=True) / width + 1e-06)
    here = pl.ds(pl.multiple_of(f * cols, 128), cols)
    normed = (stream[:, here].astype(f32) * inv * gain[:, here]).astype(bf16).astype(f32)
    slots = WAVE_EXPERTS * CAPACITY
    lane = lax.broadcasted_iota(jnp.int32, (toks, 128), 1)
    row = lax.broadcasted_iota(jnp.int32, (toks, 128), 0)
    lane_expert = lane // CAPACITY
    hits = jnp.zeros((toks, 128), f32)
    weight_of = jnp.zeros((toks, 128), f32)
    route_vals = routes[...]
    gate_vals = gates[...]
    for j in range(routes.shape[1]):
        match = route_vals[:, j : j + 1] == lane_expert
        hits = hits + jnp.where(match, 1.0, 0.0)
        weight_of = weight_of + jnp.where(match, gate_vals[:, j : j + 1], 0.0)
    rank = jnp.zeros((toks, 128), f32) - 1.0
    for t in range(toks):
        rank = rank + jnp.where(row >= t, hits[t : t + 1, :], 0.0)
    slot_of = (lane % CAPACITY).astype(f32)
    placed = jnp.where((hits == 1.0) & (rank == slot_of), 1.0, 0.0)
    mix = placed * weight_of
    for r in range(slots):
        rows_out[r // CAPACITY, r % CAPACITY : r % CAPACITY + 1, :] = jnp.sum(
            placed[:, r : r + 1] * normed, axis=0, keepdims=True
        )
    rows_in[s] = rows_out[s]

    pl.semaphore_wait(barrier, n_seq - 1 + GROUP - 1)

    rows_c, proj_c = [], []
    for k in range(1, n_seq):
        to = lax.rem(s + k, n_seq)
        rows_c.append(remote(rows_out.at[to], rows_in.at[s], rows_s.at[k], rows_r.at[k], to, f))
        rows_c[-1].start()
    for k in range(1, n_seq):
        to = lax.rem(s + k, n_seq)
        start = pl.multiple_of((to * GROUP + f) * chunk_cols, 128)
        proj_c.append(
            remote(proj.at[:, pl.ds(start, chunk_cols)], gath.at[s],
                   proj_s.at[k], proj_r.at[k], to, f)
        )
        proj_c[-1].start()

    for c in rows_c:
        c.wait_recv()
    rows = jnp.concatenate([rows_in[i] for i in range(n_seq)], axis=0).astype(bf16)
    loads[0].wait()
    loads[1].wait()
    part_c = []
    for x in (3, 2, 1, 0):
        block = pl.ds(pl.multiple_of(peers[x] * quarter, 128), quarter)
        part[x, :, :quarter] = jnp.dot(rows, gate_v[:, block], preferred_element_type=f32)
        part[x, :, quarter:] = jnp.dot(rows, up_v[:, block], preferred_element_type=f32)
        if x:
            c = remote(part.at[x], part_in.at[x], part_s.at[x], part_r.at[x], s, peers[x])
            c.start()
            part_c.append(c)

    own_proj.wait()
    for c in proj_c:
        c.wait_recv()
    for h in range(heads):
        base = h * pack
        q = gath[:, :, base : base + QK_DIM].astype(f32).reshape(span, QK_DIM)
        q_buf[f, h] = q.astype(bf16)
        wide = gath[:, :, base + 128 : base + 384].astype(f32).reshape(span, 256)
        k_span[h] = pltpu.roll(wide, 256 - (QK_DIM - 128), 1)[:, :QK_DIM].astype(bf16)
        v = gath[:, :, base + 2 * QK_DIM : base + pack].astype(f32).reshape(span, V_DIM)
        v_span[h] = v.astype(bf16)
    q_c = []
    for x in (2, 1):
        q_c.append(remote(q_buf.at[f], q_buf.at[f], q_s.at[x], q_r.at[x], s, peers[x]))
        q_c[-1].start()

    nt = (((1,), (1,)), ((), ()))
    st_lane = lax.broadcasted_iota(jnp.int32, (span, 128), 1)

    def attend(x):
        cache_loads[x].wait()

        def one_head(h, stats):
            head = peers[x] * heads + h
            q = q_buf[peers[x], h]
            scores = jnp.dot(q, cache_v[head, :QK_DIM, :], preferred_element_type=f32)
            top = jnp.max(scores, axis=1, keepdims=True)
            if x == 0:
                near = lax.dot_general(q, k_span[h], nt, preferred_element_type=f32)
                open_at = lax.broadcasted_iota(
                    jnp.int32, (span, span), 1
                ) <= lax.broadcasted_iota(jnp.int32, (span, span), 0)
                near = jnp.where(open_at, near, -jnp.inf)
                top = jnp.maximum(top, jnp.max(near, axis=1, keepdims=True))
            expw = jnp.exp2((scores - top) * scale2)
            total = jnp.sum(expw, axis=1, keepdims=True)
            out = lax.dot_general(
                expw.astype(bf16), cache_v[head, QK_DIM:, :], nt, preferred_element_type=f32
            )
            if x == 0:
                near_w = jnp.exp2((near - top) * scale2)
                total = total + jnp.sum(near_w, axis=1, keepdims=True)
                out = out + jnp.dot(near_w.astype(bf16), v_span[h], preferred_element_type=f32)
            out = out / total
            if x == 0:
                o_own[h] = out
            else:
                o_buf[x, h] = out.astype(bf16)
            stats = jnp.where(st_lane == h, top, stats)
            return jnp.where(st_lane == heads + h, total, stats)

        st_buf[x] = lax.fori_loop(0, heads, one_head, jnp.zeros((span, 128), f32))
        if x:
            pair = [
                remote(o_buf.at[x], o_in.at[x], o_s.at[x], o_r.at[x], s, peers[x]),
                remote(st_buf.at[x], st_in.at[x], st_s.at[x], st_r.at[x], s, peers[x]),
            ]
            for c in pair:
                c.start()
            return pair
        return []

    attend(0)

    for c in part_c:
        c.wait_recv()
    both = part[0] + part_in[1] + part_in[2] + part_in[3]
    gate_act = both[:, :quarter]
    hid[f] = (gate_act / (1.0 + jnp.exp(-gate_act)) * both[:, quarter:]).astype(bf16)
    hid_c = []
    for x in (3, 2, 1):
        hid_c.append(remote(hid.at[f], hid.at[f], hid_s.at[x], hid_r.at[x], s, peers[x]))
        hid_c[-1].start()

    q_c[0].wait_recv()
    q_c.append(remote(q_buf.at[f2], q_buf.at[f2], q_s.at[3], q_r.at[3], s, f1))
    q_c[-1].start()
    q_c[1].wait_recv()
    o_c = attend(1)

    for c in hid_c:
        c.wait_recv()
    loads[2].wait()
    acc = jnp.zeros((n_seq * CAPACITY, cols), f32)
    for j in range(GROUP):
        acc = acc + jnp.dot(
            hid[j], down_v[j * quarter : (j + 1) * quarter, :], preferred_element_type=f32
        )
    acc = acc.astype(bf16).astype(f32)
    for i in range(n_seq):
        down_out[i] = acc[i * CAPACITY : (i + 1) * CAPACITY, :]
    down_in[s] = down_out[s]
    dn_c = []
    for k in range(1, n_seq):
        to = lax.rem(s + k, n_seq)
        dn_c.append(remote(down_out.at[to], down_in.at[s], dn_s.at[k], dn_r.at[k], to, f))
        dn_c[-1].start()

    o_c += attend(2)
    q_c[2].wait_recv()
    o_c += attend(3)

    for c in dn_c:
        c.wait_recv()
    mixed = jnp.zeros((toks, cols), f32)
    for r in range(slots):
        mixed = mixed + mix[:, r : r + 1] * down_in[
            r // CAPACITY, r % CAPACITY : r % CAPACITY + 1, :
        ]
    routed_out[...] = mixed.astype(bf16)

    for c in o_c:
        c.wait_recv()
    stat = [st_buf[0]] + [st_in[x] for x in (1, 2, 3)]
    for h in range(heads):
        tops = [v[:, h : h + 1] for v in stat]
        totals = [v[:, heads + h : heads + h + 1] for v in stat]
        top = jnp.maximum(jnp.maximum(tops[0], tops[1]), jnp.maximum(tops[2], tops[3]))
        share = [t * jnp.exp2((m - top) * scale2) for t, m in zip(totals, tops)]
        whole = share[0] + share[1] + share[2] + share[3]
        out = o_own[h] * share[0]
        for x in (1, 2, 3):
            out = out + o_in[x, h].astype(f32) * share[x]
        out = (out / whole).reshape(n_seq, toks, V_DIM).astype(bf16)
        fin[:, :, h * V_DIM : (h + 1) * V_DIM] = out
    hop[f, s] = fin[s]
    fin_c, hop_c = [], []
    for k in range(1, n_seq):
        to = lax.rem(s + k, n_seq)
        fin_c.append(remote(fin.at[to], hop.at[f, s], fin_s.at[k], fin_r.at[k], to, f))
        fin_c[-1].start()
    for c in fin_c:
        c.wait_recv()
    for x in (3, 2, 1):
        hop_c.append(remote(hop.at[f], hop.at[f], hop_s.at[x], hop_r.at[x], s, peers[x]))
        hop_c[-1].start()
    for c in hop_c:
        c.wait_recv()
    block = heads * V_DIM
    for r in range(n_seq):
        for j in range(GROUP):
            at = (r * GROUP + j) * block
            att_out[:, at : at + block] = hop[j, r]
    for c in rows_c + proj_c + part_c + q_c + hid_c + dn_c + o_c + fin_c + hop_c:
        c.wait_send()


def fused(
    n_seq, projected, cached, stream, norm_gain, routes, route_gates, gate_weight, up_weight,
    down_weight,
):
    f32, bf16 = jnp.float32, jnp.bfloat16
    toks = stream.shape[0]
    span = n_seq * toks
    heads = cached.shape[0] // GROUP
    cols = down_weight.shape[1]
    quarter = gate_weight.shape[1] // GROUP
    slots = n_seq * CAPACITY
    vmem = pl.BlockSpec(memory_space=pltpu.VMEM)
    hbm = pl.BlockSpec(memory_space=pl.ANY)
    dma = pltpu.SemaphoreType.DMA
    scratch = [
        pltpu.VMEM((n_seq, toks, heads * (2 * QK_DIM + V_DIM)), bf16),
        pltpu.VMEM((GROUP, heads, span, QK_DIM), bf16),
        pltpu.VMEM((heads, span, QK_DIM), bf16),
        pltpu.VMEM((heads, span, V_DIM), bf16),
        pltpu.VMEM(cached.shape, bf16),
        pltpu.VMEM(gate_weight.shape, bf16),
        pltpu.VMEM(up_weight.shape, bf16),
        pltpu.VMEM(down_weight.shape, bf16),
        pltpu.VMEM((n_seq, CAPACITY, cols), f32),
        pltpu.VMEM((n_seq, CAPACITY, cols), f32),
        pltpu.VMEM((GROUP, slots, 2 * quarter), f32),
        pltpu.VMEM((GROUP, slots, 2 * quarter), f32),
        pltpu.VMEM((GROUP, slots, quarter), bf16),
        pltpu.VMEM((n_seq, CAPACITY, cols), f32),
        pltpu.VMEM((n_seq, CAPACITY, cols), f32),
        pltpu.VMEM((heads, span, V_DIM), f32),
        pltpu.VMEM((GROUP, heads, span, V_DIM), bf16),
        pltpu.VMEM((GROUP, heads, span, V_DIM), bf16),
        pltpu.VMEM((GROUP, span, 128), f32),
        pltpu.VMEM((GROUP, span, 128), f32),
        pltpu.VMEM((n_seq, toks, heads * V_DIM), bf16),
        pltpu.VMEM((GROUP, n_seq, toks, heads * V_DIM), bf16),
        dma((3 + GROUP,)),
        dma,
        dma((n_seq,)), dma((n_seq,)), dma((n_seq,)), dma((n_seq,)),
        dma((GROUP,)), dma((GROUP,)), dma((GROUP,)), dma((GROUP,)),
        dma((GROUP,)), dma((GROUP,)),
        dma((n_seq,)), dma((n_seq,)),
        dma((GROUP,)), dma((GROUP,)), dma((GROUP,)), dma((GROUP,)),
        dma((n_seq,)), dma((n_seq,)), dma((GROUP,)), dma((GROUP,)),
    ]
    return pl.pallas_call(
        functools.partial(one_kernel, n_seq),
        out_shape=(
            jax.ShapeDtypeStruct((toks, cached.shape[0] * n_seq * V_DIM), bf16),
            jax.ShapeDtypeStruct((toks, cols), bf16),
        ),
        in_specs=[hbm, hbm, vmem, vmem, vmem, vmem, hbm, hbm, hbm],
        out_specs=(vmem, vmem),
        scratch_shapes=scratch,
        compiler_params=pltpu.CompilerParams(
            collective_id=0, has_side_effects=True, vmem_limit_bytes=58 * 1024 * 1024
        ),
        cost_estimate=pl.CostEstimate(
            flops=2_000_000_000, bytes_accessed=42_000_000, transcendentals=2_000_000
        ),
    )(
        projected, cached, stream, norm_gain.reshape(1, -1), routes, route_gates,
        gate_weight, up_weight, down_weight,
    )


def fits(mesh, projected, cached):
    n_seq, n_fsdp = mesh.shape["seq"], mesh.shape["fsdp"]
    return (
        n_seq == WAVE_EXPERTS
        and n_fsdp == GROUP
        and projected.shape[0] == 8 * n_seq
        and cached.shape[0] == 16 * n_seq
        and cached.shape[2] == 1792 * n_fsdp
    )


def solution(mesh):
    placed = (
        P("seq", None),
        P("seq", None, "fsdp"),
        P("seq", None),
        P(),
        P("seq", None),
        P("seq", None),
        P("fsdp", "seq"),
        P("fsdp", "seq"),
        P("seq", "fsdp"),
    )
    outs = (P("seq", None), P("seq", "fsdp"))

    def program(projected, cached, *others):
        if fits(mesh, projected, cached):
            body = functools.partial(fused, mesh.shape["seq"])
        else:
            body = on_device
        mapped = jax.shard_map(body, mesh=mesh, in_specs=placed, out_specs=outs, check_vma=False)
        return mapped(projected, cached, *others)

    return program
```

```python
import functools
import math

import jax
import jax.numpy as jnp
from jax import lax
from jax.experimental import pallas as pl
from jax.experimental.pallas import tpu as pltpu
from jax.sharding import PartitionSpec as P

QK_DIM = 192
V_DIM = 128
WAVE_EXPERTS = 8
CAPACITY = 2


def on_device(
    projected, cached, stream, norm_gain, routes, route_gates, gate_weight, up_weight, down_weight
):
    pack_width = 2 * QK_DIM + V_DIM
    heads_here = cached.shape[0]
    cache_len = cached.shape[2]
    gathered = lax.all_to_all(projected, "seq", split_axis=1, concat_axis=0, tiled=True)
    span_len = gathered.shape[0]
    heads_major = jnp.transpose(gathered.reshape(span_len, heads_here, pack_width), (1, 0, 2))
    quarter = span_len // lax.axis_size("fsdp")
    first_key = lax.axis_index("fsdp") * quarter
    rows_block = math.gcd(512, span_len)
    block_count = span_len // rows_block
    score_scale = 1.0 / math.sqrt(QK_DIM)
    contract = (((1,), (1,)), ((), ()))

    def head_scores(head_pair):
        stacked, stored = head_pair
        key_rows = lax.dynamic_slice_in_dim(stacked[:, QK_DIM : 2 * QK_DIM], first_key, quarter, 0)
        query_blocks = stacked[:, :QK_DIM].reshape(block_count, rows_block, QK_DIM)

        def one_block(queries):
            span_scores = (
                lax.dot_general(queries, key_rows, contract, preferred_element_type=jnp.float32)
                * score_scale
            )
            cache_scores = (
                jnp.dot(queries, stored[:QK_DIM], preferred_element_type=jnp.float32) * score_scale
            )
            return jnp.concatenate([span_scores, cache_scores], axis=1)

        return lax.map(one_block, query_blocks).reshape(span_len, quarter + cache_len)

    scores = lax.map(head_scores, (heads_major, cached))
    query_pos = jnp.arange(span_len, dtype=jnp.int32)
    key_pos = first_key + jnp.arange(quarter, dtype=jnp.int32)
    span_open = key_pos[None, :] <= query_pos[:, None]
    open_mask = jnp.concatenate([span_open, jnp.ones((span_len, cache_len), bool)], axis=1)
    scores = jnp.where(open_mask[None], scores, -jnp.inf)
    highest = lax.pmax(jnp.max(scores, axis=2), "fsdp")
    exp_weights = jnp.where(open_mask[None], jnp.exp(scores - highest[:, :, None]), 0.0)
    key_total = jnp.sum(exp_weights, axis=2)
    weights_bf = exp_weights.astype(jnp.bfloat16)

    def head_values(head_item):
        weights_row, stacked, stored = head_item
        value_rows = lax.dynamic_slice_in_dim(stacked[:, 2 * QK_DIM :], first_key, quarter, 0)
        span_part = jnp.dot(
            weights_row[:, :quarter], value_rows, preferred_element_type=jnp.float32
        )
        cache_part = lax.dot_general(
            weights_row[:, quarter:], stored[QK_DIM:], contract, preferred_element_type=jnp.float32
        )
        return span_part + cache_part

    weighted = lax.map(head_values, (weights_bf, heads_major, cached))
    weighted, key_total = lax.psum((weighted, key_total), "fsdp")
    outputs = (weighted / key_total[:, :, None]).astype(jnp.bfloat16)
    merged = jnp.transpose(outputs, (1, 0, 2)).reshape(span_len, heads_here * V_DIM)
    attention = lax.all_to_all(merged, "seq", split_axis=0, concat_axis=1, tiled=True)
    tokens = stream.astype(jnp.float32)
    tok_count = tokens.shape[0]
    slice_cols = gate_weight.shape[0]
    normed = (
        tokens * lax.rsqrt(jnp.mean(tokens * tokens, axis=1, keepdims=True) + 1e-06) * norm_gain
    ).astype(jnp.bfloat16)
    experts_here = jnp.arange(WAVE_EXPERTS, dtype=jnp.int32)
    matches = routes[:, :, None] == experts_here[None, None, :]
    hit_counts = jnp.sum(matches.astype(jnp.int32), axis=1)
    weight_of = jnp.sum(jnp.where(matches, route_gates[:, :, None], 0.0), axis=1)
    rank_rows = jnp.cumsum(hit_counts, axis=0) - 1
    slot_ids = jnp.arange(CAPACITY, dtype=jnp.int32)
    placed = (hit_counts[None, :, :] == 1) & (rank_rows[None, :, :] == slot_ids[:, None, None])
    placed = jnp.transpose(placed, (2, 0, 1)).astype(jnp.float32)
    slot_weight = jnp.einsum("ect,te->ec", placed, weight_of, precision=lax.Precision.HIGHEST)
    placed_flat = placed.reshape(WAVE_EXPERTS * CAPACITY, tok_count)
    send_rows = jnp.dot(
        placed_flat.astype(jnp.bfloat16), normed, preferred_element_type=jnp.float32
    ).astype(jnp.bfloat16)
    group_size = lax.axis_size("seq") // WAVE_EXPERTS
    send_rows = lax.dynamic_slice_in_dim(
        send_rows, lax.axis_index("fsdp") * slice_cols, slice_cols, 1
    )
    outgoing = jnp.broadcast_to(
        send_rows.reshape(WAVE_EXPERTS, 1, CAPACITY, slice_cols),
        (WAVE_EXPERTS, group_size, CAPACITY, slice_cols),
    )
    outgoing = outgoing.reshape(WAVE_EXPERTS * group_size, CAPACITY, slice_cols)
    received = lax.all_to_all(outgoing, "seq", split_axis=0, concat_axis=0, tiled=True)
    rows_in = received.reshape(-1, received.shape[2])
    gate_act = jnp.dot(rows_in, gate_weight, preferred_element_type=jnp.float32)
    upward = jnp.dot(rows_in, up_weight, preferred_element_type=jnp.float32)
    gate_act, upward = lax.psum((gate_act, upward), "fsdp")
    hidden = (jax.nn.silu(gate_act) * upward).astype(jnp.bfloat16)
    partial_value = jnp.dot(hidden, down_weight, preferred_element_type=jnp.float32).astype(
        jnp.bfloat16
    )
    partial_value = partial_value.reshape(received.shape[0], received.shape[1], slice_cols)
    result = lax.all_to_all(partial_value, "seq", split_axis=0, concat_axis=0, tiled=True)
    expert_out = jnp.sum(
        result.reshape(WAVE_EXPERTS, group_size, CAPACITY, slice_cols).astype(jnp.float32), axis=1
    )
    weighted_out = expert_out * slot_weight[:, :, None]
    mixed_rows = lax.dot_general(
        placed_flat,
        weighted_out.reshape(WAVE_EXPERTS * CAPACITY, slice_cols),
        (((0,), (0,)), ((), ())),
        precision=lax.Precision.HIGHEST,
    )
    routed = mixed_rows.astype(jnp.bfloat16)
    return (attention, routed)


MESH = pl.DeviceIdType.MESH
GROUP = 4
LOG2E = 1.4426950408889634


def one_kernel(
    n_seq,
    proj, cached, stream, gain, routes, gates, gate_w, up_w, down_w,
    att_out, routed_out,
    gath, q_buf, k_span, v_span, cache_v, gate_v, up_v, down_v,
    rows_out, rows_in, part, part_in, hid, down_out, down_in,
    o_own, o_buf, o_in, st_buf, st_in, fin, hop,
    load_sem, own_sem,
    rows_s, rows_r, proj_s, proj_r, q_s, q_r, part_s, part_r, hid_s, hid_r,
    dn_s, dn_r, o_s, o_r, st_s, st_r, fin_s, fin_r, hop_s, hop_r,
):
    f32, bf16 = jnp.float32, jnp.bfloat16
    s = lax.axis_index("seq")
    f = lax.axis_index("fsdp")
    f1 = f + 1 - 2 * lax.rem(f, 2)
    f2 = lax.rem(f + 2, 4)
    f3 = lax.rem(f1 + 2, 4)
    peers = (f, f1, f2, f3)
    width = stream.shape[1]
    cols = down_w.shape[1]
    heads = cached.shape[0] // GROUP
    pack = 2 * QK_DIM + V_DIM
    chunk_cols = heads * pack
    quarter = gate_w.shape[1] // GROUP
    toks = stream.shape[0]
    span = n_seq * toks
    scale2 = LOG2E / math.sqrt(QK_DIM)

    def remote(src, dst, ssem, rsem, seq_id, fs_id):
        return pltpu.make_async_remote_copy(
            src_ref=src, dst_ref=dst, send_sem=ssem, recv_sem=rsem,
            device_id=(seq_id, fs_id), device_id_type=MESH,
        )

    own_proj = pltpu.make_async_copy(
        proj.at[:, pl.ds(pl.multiple_of((s * GROUP + f) * chunk_cols, 128), chunk_cols)],
        gath.at[s], own_sem,
    )
    own_proj.start()
    loads = [
        pltpu.make_async_copy(gate_w, gate_v, load_sem.at[0]),
        pltpu.make_async_copy(up_w, up_v, load_sem.at[1]),
        pltpu.make_async_copy(down_w, down_v, load_sem.at[2]),
    ]
    cache_loads = []
    for x in range(GROUP):
        piece = pl.ds(peers[x] * heads, heads)
        cache_loads.append(
            pltpu.make_async_copy(cached.at[piece], cache_v.at[piece], load_sem.at[3 + x])
        )
    for copy in (loads[0], loads[1], cache_loads[0], cache_loads[1], loads[2],
                 cache_loads[2], cache_loads[3]):
        copy.start()

    barrier = pltpu.get_barrier_semaphore()
    for k in range(1, n_seq):
        pl.semaphore_signal(
            barrier, inc=1, device_id=(lax.rem(s + k, n_seq), f), device_id_type=MESH
        )
    for x in range(1, GROUP):
        pl.semaphore_signal(barrier, inc=1, device_id=(s, peers[x]), device_id_type=MESH)

    tokens = stream[...].astype(f32)
    inv = lax.rsqrt(jnp.sum(tokens * tokens, axis=1, keepdims=True) / width + 1e-06)
    here = pl.ds(pl.multiple_of(f * cols, 128), cols)
    normed = (stream[:, here].astype(f32) * inv * gain[:, here]).astype(bf16).astype(f32)
    slots = WAVE_EXPERTS * CAPACITY
    lane = lax.broadcasted_iota(jnp.int32, (toks, 128), 1)
    row = lax.broadcasted_iota(jnp.int32, (toks, 128), 0)
    lane_expert = lane // CAPACITY
    hits = jnp.zeros((toks, 128), f32)
    weight_of = jnp.zeros((toks, 128), f32)
    route_vals = routes[...]
    gate_vals = gates[...]
    for j in range(routes.shape[1]):
        match = route_vals[:, j : j + 1] == lane_expert
        hits = hits + jnp.where(match, 1.0, 0.0)
        weight_of = weight_of + jnp.where(match, gate_vals[:, j : j + 1], 0.0)
    rank = jnp.zeros((toks, 128), f32) - 1.0
    for t in range(toks):
        rank = rank + jnp.where(row >= t, hits[t : t + 1, :], 0.0)
    slot_of = (lane % CAPACITY).astype(f32)
    placed = jnp.where((hits == 1.0) & (rank == slot_of), 1.0, 0.0)
    mix = placed * weight_of
    for r in range(slots):
        rows_out[r // CAPACITY, r % CAPACITY : r % CAPACITY + 1, :] = jnp.sum(
            placed[:, r : r + 1] * normed, axis=0, keepdims=True
        )
    rows_in[s] = rows_out[s]

    pl.semaphore_wait(barrier, n_seq - 1 + GROUP - 1)

    rows_c, proj_c = [], []
    for k in range(1, n_seq):
        to = lax.rem(s + k, n_seq)
        rows_c.append(remote(rows_out.at[to], rows_in.at[s], rows_s.at[k], rows_r.at[k], to, f))
        rows_c[-1].start()
    for k in range(1, n_seq):
        to = lax.rem(s + k, n_seq)
        start = pl.multiple_of((to * GROUP + f) * chunk_cols, 128)
        proj_c.append(
            remote(proj.at[:, pl.ds(start, chunk_cols)], gath.at[s],
                   proj_s.at[k], proj_r.at[k], to, f)
        )
        proj_c[-1].start()

    for c in rows_c:
        c.wait_recv()
    rows = jnp.concatenate([rows_in[i] for i in range(n_seq)], axis=0).astype(bf16)
    loads[0].wait()
    loads[1].wait()
    part_c = []
    for x in (3, 2, 1, 0):
        block = pl.ds(pl.multiple_of(peers[x] * quarter, 128), quarter)
        part[x, :, :quarter] = jnp.dot(rows, gate_v[:, block], preferred_element_type=f32)
        part[x, :, quarter:] = jnp.dot(rows, up_v[:, block], preferred_element_type=f32)
        if x:
            c = remote(part.at[x], part_in.at[x], part_s.at[x], part_r.at[x], s, peers[x])
            c.start()
            part_c.append(c)

    own_proj.wait()
    for c in proj_c:
        c.wait_recv()
    for h in range(heads):
        base = h * pack
        q = gath[:, :, base : base + QK_DIM].astype(f32).reshape(span, QK_DIM)
        q_buf[f, h] = q.astype(bf16)
        wide = gath[:, :, base + 128 : base + 384].astype(f32).reshape(span, 256)
        k_span[h] = pltpu.roll(wide, 256 - (QK_DIM - 128), 1)[:, :QK_DIM].astype(bf16)
        v = gath[:, :, base + 2 * QK_DIM : base + pack].astype(f32).reshape(span, V_DIM)
        v_span[h] = v.astype(bf16)
    q_c = []
    for x in (2, 1):
        q_c.append(remote(q_buf.at[f], q_buf.at[f], q_s.at[x], q_r.at[x], s, peers[x]))
        q_c[-1].start()

    nt = (((1,), (1,)), ((), ()))
    st_lane = lax.broadcasted_iota(jnp.int32, (span, 128), 1)

    def attend(x):
        cache_loads[x].wait()

        def one_head(h, stats):
            head = peers[x] * heads + h
            q = q_buf[peers[x], h]
            scores = jnp.dot(q, cache_v[head, :QK_DIM, :], preferred_element_type=f32)
            top = jnp.max(scores, axis=1, keepdims=True)
            if x == 0:
                near = lax.dot_general(q, k_span[h], nt, preferred_element_type=f32)
                open_at = lax.broadcasted_iota(
                    jnp.int32, (span, span), 1
                ) <= lax.broadcasted_iota(jnp.int32, (span, span), 0)
                near = jnp.where(open_at, near, -jnp.inf)
                top = jnp.maximum(top, jnp.max(near, axis=1, keepdims=True))
            expw = jnp.exp2((scores - top) * scale2)
            total = jnp.sum(expw, axis=1, keepdims=True)
            out = lax.dot_general(
                expw.astype(bf16), cache_v[head, QK_DIM:, :], nt, preferred_element_type=f32
            )
            if x == 0:
                near_w = jnp.exp2((near - top) * scale2)
                total = total + jnp.sum(near_w, axis=1, keepdims=True)
                out = out + jnp.dot(near_w.astype(bf16), v_span[h], preferred_element_type=f32)
            out = out / total
            if x == 0:
                o_own[h] = out
            else:
                o_buf[x, h] = out.astype(bf16)
            stats = jnp.where(st_lane == h, top, stats)
            return jnp.where(st_lane == heads + h, total, stats)

        st_buf[x] = lax.fori_loop(
            0, heads, one_head, jnp.zeros((span, 128), f32), unroll=True
        )
        if x:
            pair = [
                remote(o_buf.at[x], o_in.at[x], o_s.at[x], o_r.at[x], s, peers[x]),
                remote(st_buf.at[x], st_in.at[x], st_s.at[x], st_r.at[x], s, peers[x]),
            ]
            for c in pair:
                c.start()
            return pair
        return []

    attend(0)

    for c in part_c:
        c.wait_recv()
    both = part[0] + part_in[1] + part_in[2] + part_in[3]
    gate_act = both[:, :quarter]
    hid[f] = (gate_act / (1.0 + jnp.exp(-gate_act)) * both[:, quarter:]).astype(bf16)
    hid_c = []
    for x in (3, 2, 1):
        hid_c.append(remote(hid.at[f], hid.at[f], hid_s.at[x], hid_r.at[x], s, peers[x]))
        hid_c[-1].start()

    q_c[0].wait_recv()
    q_c.append(remote(q_buf.at[f2], q_buf.at[f2], q_s.at[3], q_r.at[3], s, f1))
    q_c[-1].start()
    q_c[1].wait_recv()
    o_c = attend(1)

    for c in hid_c:
        c.wait_recv()
    loads[2].wait()
    acc = jnp.zeros((n_seq * CAPACITY, cols), f32)
    for j in range(GROUP):
        acc = acc + jnp.dot(
            hid[j], down_v[j * quarter : (j + 1) * quarter, :], preferred_element_type=f32
        )
    acc = acc.astype(bf16).astype(f32)
    for i in range(n_seq):
        down_out[i] = acc[i * CAPACITY : (i + 1) * CAPACITY, :]
    down_in[s] = down_out[s]
    dn_c = []
    for k in range(1, n_seq):
        to = lax.rem(s + k, n_seq)
        dn_c.append(remote(down_out.at[to], down_in.at[s], dn_s.at[k], dn_r.at[k], to, f))
        dn_c[-1].start()

    o_c += attend(2)
    q_c[2].wait_recv()
    o_c += attend(3)

    for c in dn_c:
        c.wait_recv()
    mixed = jnp.zeros((toks, cols), f32)
    for r in range(slots):
        mixed = mixed + mix[:, r : r + 1] * down_in[
            r // CAPACITY, r % CAPACITY : r % CAPACITY + 1, :
        ]
    routed_out[...] = mixed.astype(bf16)

    for c in o_c:
        c.wait_recv()
    stat = [st_buf[0]] + [st_in[x] for x in (1, 2, 3)]
    for h in range(heads):
        tops = [v[:, h : h + 1] for v in stat]
        totals = [v[:, heads + h : heads + h + 1] for v in stat]
        top = jnp.maximum(jnp.maximum(tops[0], tops[1]), jnp.maximum(tops[2], tops[3]))
        share = [t * jnp.exp2((m - top) * scale2) for t, m in zip(totals, tops)]
        whole = share[0] + share[1] + share[2] + share[3]
        out = o_own[h] * share[0]
        for x in (1, 2, 3):
            out = out + o_in[x, h].astype(f32) * share[x]
        out = (out / whole).reshape(n_seq, toks, V_DIM).astype(bf16)
        fin[:, :, h * V_DIM : (h + 1) * V_DIM] = out
    hop[f, s] = fin[s]
    fin_c, hop_c = [], []
    for k in range(1, n_seq):
        to = lax.rem(s + k, n_seq)
        fin_c.append(remote(fin.at[to], hop.at[f, s], fin_s.at[k], fin_r.at[k], to, f))
        fin_c[-1].start()
    for c in fin_c:
        c.wait_recv()
    for x in (3, 2, 1):
        hop_c.append(remote(hop.at[f], hop.at[f], hop_s.at[x], hop_r.at[x], s, peers[x]))
        hop_c[-1].start()
    for c in hop_c:
        c.wait_recv()
    block = heads * V_DIM
    for r in range(n_seq):
        for j in range(GROUP):
            at = (r * GROUP + j) * block
            att_out[:, at : at + block] = hop[j, r]
    for c in rows_c + proj_c + part_c + q_c + hid_c + dn_c + o_c + fin_c + hop_c:
        c.wait_send()


def fused(
    n_seq, projected, cached, stream, norm_gain, routes, route_gates, gate_weight, up_weight,
    down_weight,
):
    f32, bf16 = jnp.float32, jnp.bfloat16
    toks = stream.shape[0]
    span = n_seq * toks
    heads = cached.shape[0] // GROUP
    cols = down_weight.shape[1]
    quarter = gate_weight.shape[1] // GROUP
    slots = n_seq * CAPACITY
    vmem = pl.BlockSpec(memory_space=pltpu.VMEM)
    hbm = pl.BlockSpec(memory_space=pl.ANY)
    dma = pltpu.SemaphoreType.DMA
    scratch = [
        pltpu.VMEM((n_seq, toks, heads * (2 * QK_DIM + V_DIM)), bf16),
        pltpu.VMEM((GROUP, heads, span, QK_DIM), bf16),
        pltpu.VMEM((heads, span, QK_DIM), bf16),
        pltpu.VMEM((heads, span, V_DIM), bf16),
        pltpu.VMEM(cached.shape, bf16),
        pltpu.VMEM(gate_weight.shape, bf16),
        pltpu.VMEM(up_weight.shape, bf16),
        pltpu.VMEM(down_weight.shape, bf16),
        pltpu.VMEM((n_seq, CAPACITY, cols), f32),
        pltpu.VMEM((n_seq, CAPACITY, cols), f32),
        pltpu.VMEM((GROUP, slots, 2 * quarter), f32),
        pltpu.VMEM((GROUP, slots, 2 * quarter), f32),
        pltpu.VMEM((GROUP, slots, quarter), bf16),
        pltpu.VMEM((n_seq, CAPACITY, cols), f32),
        pltpu.VMEM((n_seq, CAPACITY, cols), f32),
        pltpu.VMEM((heads, span, V_DIM), f32),
        pltpu.VMEM((GROUP, heads, span, V_DIM), bf16),
        pltpu.VMEM((GROUP, heads, span, V_DIM), bf16),
        pltpu.VMEM((GROUP, span, 128), f32),
        pltpu.VMEM((GROUP, span, 128), f32),
        pltpu.VMEM((n_seq, toks, heads * V_DIM), bf16),
        pltpu.VMEM((GROUP, n_seq, toks, heads * V_DIM), bf16),
        dma((3 + GROUP,)),
        dma,
        dma((n_seq,)), dma((n_seq,)), dma((n_seq,)), dma((n_seq,)),
        dma((GROUP,)), dma((GROUP,)), dma((GROUP,)), dma((GROUP,)),
        dma((GROUP,)), dma((GROUP,)),
        dma((n_seq,)), dma((n_seq,)),
        dma((GROUP,)), dma((GROUP,)), dma((GROUP,)), dma((GROUP,)),
        dma((n_seq,)), dma((n_seq,)), dma((GROUP,)), dma((GROUP,)),
    ]
    return pl.pallas_call(
        functools.partial(one_kernel, n_seq),
        out_shape=(
            jax.ShapeDtypeStruct((toks, cached.shape[0] * n_seq * V_DIM), bf16),
            jax.ShapeDtypeStruct((toks, cols), bf16),
        ),
        in_specs=[hbm, hbm, vmem, vmem, vmem, vmem, hbm, hbm, hbm],
        out_specs=(vmem, vmem),
        scratch_shapes=scratch,
        compiler_params=pltpu.CompilerParams(
            collective_id=0, has_side_effects=True, vmem_limit_bytes=58 * 1024 * 1024
        ),
        cost_estimate=pl.CostEstimate(
            flops=2_000_000_000, bytes_accessed=42_000_000, transcendentals=2_000_000
        ),
    )(
        projected, cached, stream, norm_gain.reshape(1, -1), routes, route_gates,
        gate_weight, up_weight, down_weight,
    )


def fits(mesh, projected, cached):
    n_seq, n_fsdp = mesh.shape["seq"], mesh.shape["fsdp"]
    return (
        n_seq == WAVE_EXPERTS
        and n_fsdp == GROUP
        and projected.shape[0] == 8 * n_seq
        and cached.shape[0] == 16 * n_seq
        and cached.shape[2] == 1792 * n_fsdp
    )


def solution(mesh):
    placed = (
        P("seq", None),
        P("seq", None, "fsdp"),
        P("seq", None),
        P(),
        P("seq", None),
        P("seq", None),
        P("fsdp", "seq"),
        P("fsdp", "seq"),
        P("seq", "fsdp"),
    )
    outs = (P("seq", None), P("seq", "fsdp"))

    def program(projected, cached, *others):
        if fits(mesh, projected, cached):
            body = functools.partial(fused, mesh.shape["seq"])
        else:
            body = on_device
        mapped = jax.shard_map(body, mesh=mesh, in_specs=placed, out_specs=outs, check_vma=False)
        return mapped(projected, cached, *others)

    return program
```

```python
import functools
import math

import jax
import jax.numpy as jnp
from jax import lax
from jax.experimental import pallas as pl
from jax.experimental.pallas import tpu as pltpu
from jax.sharding import PartitionSpec as P

QK_DIM = 192
V_DIM = 128
WAVE_EXPERTS = 8
CAPACITY = 2


def on_device(
    projected, cached, stream, norm_gain, routes, route_gates, gate_weight, up_weight, down_weight
):
    pack_width = 2 * QK_DIM + V_DIM
    heads_here = cached.shape[0]
    cache_len = cached.shape[2]
    gathered = lax.all_to_all(projected, "seq", split_axis=1, concat_axis=0, tiled=True)
    span_len = gathered.shape[0]
    heads_major = jnp.transpose(gathered.reshape(span_len, heads_here, pack_width), (1, 0, 2))
    quarter = span_len // lax.axis_size("fsdp")
    first_key = lax.axis_index("fsdp") * quarter
    rows_block = math.gcd(512, span_len)
    block_count = span_len // rows_block
    score_scale = 1.0 / math.sqrt(QK_DIM)
    contract = (((1,), (1,)), ((), ()))

    def head_scores(head_pair):
        stacked, stored = head_pair
        key_rows = lax.dynamic_slice_in_dim(stacked[:, QK_DIM : 2 * QK_DIM], first_key, quarter, 0)
        query_blocks = stacked[:, :QK_DIM].reshape(block_count, rows_block, QK_DIM)

        def one_block(queries):
            span_scores = (
                lax.dot_general(queries, key_rows, contract, preferred_element_type=jnp.float32)
                * score_scale
            )
            cache_scores = (
                jnp.dot(queries, stored[:QK_DIM], preferred_element_type=jnp.float32) * score_scale
            )
            return jnp.concatenate([span_scores, cache_scores], axis=1)

        return lax.map(one_block, query_blocks).reshape(span_len, quarter + cache_len)

    scores = lax.map(head_scores, (heads_major, cached))
    query_pos = jnp.arange(span_len, dtype=jnp.int32)
    key_pos = first_key + jnp.arange(quarter, dtype=jnp.int32)
    span_open = key_pos[None, :] <= query_pos[:, None]
    open_mask = jnp.concatenate([span_open, jnp.ones((span_len, cache_len), bool)], axis=1)
    scores = jnp.where(open_mask[None], scores, -jnp.inf)
    highest = lax.pmax(jnp.max(scores, axis=2), "fsdp")
    exp_weights = jnp.where(open_mask[None], jnp.exp(scores - highest[:, :, None]), 0.0)
    key_total = jnp.sum(exp_weights, axis=2)
    weights_bf = exp_weights.astype(jnp.bfloat16)

    def head_values(head_item):
        weights_row, stacked, stored = head_item
        value_rows = lax.dynamic_slice_in_dim(stacked[:, 2 * QK_DIM :], first_key, quarter, 0)
        span_part = jnp.dot(
            weights_row[:, :quarter], value_rows, preferred_element_type=jnp.float32
        )
        cache_part = lax.dot_general(
            weights_row[:, quarter:], stored[QK_DIM:], contract, preferred_element_type=jnp.float32
        )
        return span_part + cache_part

    weighted = lax.map(head_values, (weights_bf, heads_major, cached))
    weighted, key_total = lax.psum((weighted, key_total), "fsdp")
    outputs = (weighted / key_total[:, :, None]).astype(jnp.bfloat16)
    merged = jnp.transpose(outputs, (1, 0, 2)).reshape(span_len, heads_here * V_DIM)
    attention = lax.all_to_all(merged, "seq", split_axis=0, concat_axis=1, tiled=True)
    tokens = stream.astype(jnp.float32)
    tok_count = tokens.shape[0]
    slice_cols = gate_weight.shape[0]
    normed = (
        tokens * lax.rsqrt(jnp.mean(tokens * tokens, axis=1, keepdims=True) + 1e-06) * norm_gain
    ).astype(jnp.bfloat16)
    experts_here = jnp.arange(WAVE_EXPERTS, dtype=jnp.int32)
    matches = routes[:, :, None] == experts_here[None, None, :]
    hit_counts = jnp.sum(matches.astype(jnp.int32), axis=1)
    weight_of = jnp.sum(jnp.where(matches, route_gates[:, :, None], 0.0), axis=1)
    rank_rows = jnp.cumsum(hit_counts, axis=0) - 1
    slot_ids = jnp.arange(CAPACITY, dtype=jnp.int32)
    placed = (hit_counts[None, :, :] == 1) & (rank_rows[None, :, :] == slot_ids[:, None, None])
    placed = jnp.transpose(placed, (2, 0, 1)).astype(jnp.float32)
    slot_weight = jnp.einsum("ect,te->ec", placed, weight_of, precision=lax.Precision.HIGHEST)
    placed_flat = placed.reshape(WAVE_EXPERTS * CAPACITY, tok_count)
    send_rows = jnp.dot(
        placed_flat.astype(jnp.bfloat16), normed, preferred_element_type=jnp.float32
    ).astype(jnp.bfloat16)
    group_size = lax.axis_size("seq") // WAVE_EXPERTS
    send_rows = lax.dynamic_slice_in_dim(
        send_rows, lax.axis_index("fsdp") * slice_cols, slice_cols, 1
    )
    outgoing = jnp.broadcast_to(
        send_rows.reshape(WAVE_EXPERTS, 1, CAPACITY, slice_cols),
        (WAVE_EXPERTS, group_size, CAPACITY, slice_cols),
    )
    outgoing = outgoing.reshape(WAVE_EXPERTS * group_size, CAPACITY, slice_cols)
    received = lax.all_to_all(outgoing, "seq", split_axis=0, concat_axis=0, tiled=True)
    rows_in = received.reshape(-1, received.shape[2])
    gate_act = jnp.dot(rows_in, gate_weight, preferred_element_type=jnp.float32)
    upward = jnp.dot(rows_in, up_weight, preferred_element_type=jnp.float32)
    gate_act, upward = lax.psum((gate_act, upward), "fsdp")
    hidden = (jax.nn.silu(gate_act) * upward).astype(jnp.bfloat16)
    partial_value = jnp.dot(hidden, down_weight, preferred_element_type=jnp.float32).astype(
        jnp.bfloat16
    )
    partial_value = partial_value.reshape(received.shape[0], received.shape[1], slice_cols)
    result = lax.all_to_all(partial_value, "seq", split_axis=0, concat_axis=0, tiled=True)
    expert_out = jnp.sum(
        result.reshape(WAVE_EXPERTS, group_size, CAPACITY, slice_cols).astype(jnp.float32), axis=1
    )
    weighted_out = expert_out * slot_weight[:, :, None]
    mixed_rows = lax.dot_general(
        placed_flat,
        weighted_out.reshape(WAVE_EXPERTS * CAPACITY, slice_cols),
        (((0,), (0,)), ((), ())),
        precision=lax.Precision.HIGHEST,
    )
    routed = mixed_rows.astype(jnp.bfloat16)
    return (attention, routed)


MESH = pl.DeviceIdType.MESH
GROUP = 4
LOG2E = 1.4426950408889634


def one_kernel(
    n_seq,
    proj, cached, stream, gain, routes, gates, gate_w, up_w, down_w,
    att_out, routed_out,
    gath, q_buf, k_span, v_span, cache_v, gate_v, up_v, down_v,
    rows_out, rows_in, part, part_in, hid, down_out, down_in,
    o_own, o_buf, o_in, st_buf, st_in, fin, hop,
    load_sem, own_sem,
    rows_s, rows_r, proj_s, proj_r, q_s, q_r, part_s, part_r, hid_s, hid_r,
    dn_s, dn_r, o_s, o_r, st_s, st_r, fin_s, fin_r, hop_s, hop_r,
):
    f32, bf16 = jnp.float32, jnp.bfloat16
    s = lax.axis_index("seq")
    f = lax.axis_index("fsdp")
    f1 = f + 1 - 2 * lax.rem(f, 2)
    f2 = lax.rem(f + 2, 4)
    f3 = lax.rem(f1 + 2, 4)
    peers = (f, f1, f2, f3)
    width = stream.shape[1]
    cols = down_w.shape[1]
    heads = cached.shape[0] // GROUP
    pack = 2 * QK_DIM + V_DIM
    chunk_cols = heads * pack
    quarter = gate_w.shape[1] // GROUP
    toks = stream.shape[0]
    span = n_seq * toks
    scale2 = LOG2E / math.sqrt(QK_DIM)

    def remote(src, dst, ssem, rsem, seq_id, fs_id):
        return pltpu.make_async_remote_copy(
            src_ref=src, dst_ref=dst, send_sem=ssem, recv_sem=rsem,
            device_id=(seq_id, fs_id), device_id_type=MESH,
        )

    own_proj = pltpu.make_async_copy(
        proj.at[:, pl.ds(pl.multiple_of((s * GROUP + f) * chunk_cols, 128), chunk_cols)],
        gath.at[s], own_sem,
    )
    own_proj.start()
    loads = [
        pltpu.make_async_copy(gate_w, gate_v, load_sem.at[0]),
        pltpu.make_async_copy(up_w, up_v, load_sem.at[1]),
        pltpu.make_async_copy(down_w, down_v, load_sem.at[2]),
    ]
    cache_loads = []
    for x in range(GROUP):
        piece = pl.ds(peers[x] * heads, heads)
        cache_loads.append(
            pltpu.make_async_copy(cached.at[piece], cache_v.at[piece], load_sem.at[3 + x])
        )
    for copy in (loads[0], loads[1], cache_loads[0], cache_loads[1], loads[2],
                 cache_loads[2], cache_loads[3]):
        copy.start()

    barrier = pltpu.get_barrier_semaphore()
    for k in range(1, n_seq):
        pl.semaphore_signal(
            barrier, inc=1, device_id=(lax.rem(s + k, n_seq), f), device_id_type=MESH
        )
    for x in range(1, GROUP):
        pl.semaphore_signal(barrier, inc=1, device_id=(s, peers[x]), device_id_type=MESH)

    tokens = stream[...].astype(f32)
    inv = lax.rsqrt(jnp.sum(tokens * tokens, axis=1, keepdims=True) / width + 1e-06)
    here = pl.ds(pl.multiple_of(f * cols, 128), cols)
    normed = (stream[:, here].astype(f32) * inv * gain[:, here]).astype(bf16).astype(f32)
    slots = WAVE_EXPERTS * CAPACITY
    lane = lax.broadcasted_iota(jnp.int32, (toks, 128), 1)
    row = lax.broadcasted_iota(jnp.int32, (toks, 128), 0)
    lane_expert = lane // CAPACITY
    hits = jnp.zeros((toks, 128), f32)
    weight_of = jnp.zeros((toks, 128), f32)
    route_vals = routes[...]
    gate_vals = gates[...]
    for j in range(routes.shape[1]):
        match = route_vals[:, j : j + 1] == lane_expert
        hits = hits + jnp.where(match, 1.0, 0.0)
        weight_of = weight_of + jnp.where(match, gate_vals[:, j : j + 1], 0.0)
    rank = jnp.zeros((toks, 128), f32) - 1.0
    for t in range(toks):
        rank = rank + jnp.where(row >= t, hits[t : t + 1, :], 0.0)
    slot_of = (lane % CAPACITY).astype(f32)
    placed = jnp.where((hits == 1.0) & (rank == slot_of), 1.0, 0.0)
    mix = placed * weight_of
    for r in range(slots):
        rows_out[r // CAPACITY, r % CAPACITY : r % CAPACITY + 1, :] = jnp.sum(
            placed[:, r : r + 1] * normed, axis=0, keepdims=True
        )
    rows_in[s] = rows_out[s]

    pl.semaphore_wait(barrier, n_seq - 1 + GROUP - 1)

    rows_c, proj_c = [], []
    for k in range(1, n_seq):
        to = lax.rem(s + k, n_seq)
        rows_c.append(remote(rows_out.at[to], rows_in.at[s], rows_s.at[k], rows_r.at[k], to, f))
        rows_c[-1].start()
    for k in range(1, n_seq):
        to = lax.rem(s + k, n_seq)
        start = pl.multiple_of((to * GROUP + f) * chunk_cols, 128)
        proj_c.append(
            remote(proj.at[:, pl.ds(start, chunk_cols)], gath.at[s],
                   proj_s.at[k], proj_r.at[k], to, f)
        )
        proj_c[-1].start()

    for c in rows_c:
        c.wait_recv()
    rows = jnp.concatenate([rows_in[i] for i in range(n_seq)], axis=0).astype(bf16)
    loads[0].wait()
    loads[1].wait()
    part_c = []
    for x in (3, 2, 1, 0):
        block = pl.ds(pl.multiple_of(peers[x] * quarter, 128), quarter)
        part[x, :, :quarter] = jnp.dot(rows, gate_v[:, block], preferred_element_type=f32)
        part[x, :, quarter:] = jnp.dot(rows, up_v[:, block], preferred_element_type=f32)
        if x:
            c = remote(part.at[x], part_in.at[x], part_s.at[x], part_r.at[x], s, peers[x])
            c.start()
            part_c.append(c)

    own_proj.wait()
    for c in proj_c:
        c.wait_recv()
    for h in range(heads):
        base = h * pack
        q = gath[:, :, base : base + QK_DIM].astype(f32).reshape(span, QK_DIM)
        q_buf[f, h] = q.astype(bf16)
        wide = gath[:, :, base + 128 : base + 384].astype(f32).reshape(span, 256)
        k_span[h] = pltpu.roll(wide, 256 - (QK_DIM - 128), 1)[:, :QK_DIM].astype(bf16)
        v = gath[:, :, base + 2 * QK_DIM : base + pack].astype(f32).reshape(span, V_DIM)
        v_span[h] = v.astype(bf16)
    q_c = []
    for x in (2, 1):
        q_c.append(remote(q_buf.at[f], q_buf.at[f], q_s.at[x], q_r.at[x], s, peers[x]))
        q_c[-1].start()

    nt = (((1,), (1,)), ((), ()))
    st_lane = lax.broadcasted_iota(jnp.int32, (span, 128), 1)

    def attend(x):
        cache_loads[x].wait()

        def one_head(h, stats):
            head = peers[x] * heads + h
            q = q_buf[peers[x], h]
            scores = jnp.dot(q, cache_v[head, :QK_DIM, :], preferred_element_type=f32)
            top = jnp.max(scores, axis=1, keepdims=True)
            if x == 0:
                near = lax.dot_general(q, k_span[h], nt, preferred_element_type=f32)
                open_at = lax.broadcasted_iota(
                    jnp.int32, (span, span), 1
                ) <= lax.broadcasted_iota(jnp.int32, (span, span), 0)
                near = jnp.where(open_at, near, -jnp.inf)
                top = jnp.maximum(top, jnp.max(near, axis=1, keepdims=True))
            expw = jnp.exp2((scores - top) * scale2)
            total = jnp.sum(expw, axis=1, keepdims=True)
            out = lax.dot_general(
                expw.astype(bf16), cache_v[head, QK_DIM:, :], nt, preferred_element_type=f32
            )
            if x == 0:
                near_w = jnp.exp2((near - top) * scale2)
                total = total + jnp.sum(near_w, axis=1, keepdims=True)
                out = out + jnp.dot(near_w.astype(bf16), v_span[h], preferred_element_type=f32)
            out = out / total
            if x == 0:
                o_own[h] = out
            else:
                o_buf[x, h] = out.astype(bf16)
            stats = jnp.where(st_lane == h, top, stats)
            return jnp.where(st_lane == heads + h, total, stats)

        st_buf[x] = lax.fori_loop(
            0, heads, one_head, jnp.zeros((span, 128), f32), unroll=True
        )
        if x:
            pair = [
                remote(o_buf.at[x], o_in.at[x], o_s.at[x], o_r.at[x], s, peers[x]),
                remote(st_buf.at[x], st_in.at[x], st_s.at[x], st_r.at[x], s, peers[x]),
            ]
            for c in pair:
                c.start()
            return pair
        return []

    attend(0)

    q_c[0].wait_recv()
    q_c.append(remote(q_buf.at[f2], q_buf.at[f2], q_s.at[3], q_r.at[3], s, f1))
    q_c[-1].start()

    for c in part_c:
        c.wait_recv()
    both = part[0] + part_in[1] + part_in[2] + part_in[3]
    gate_act = both[:, :quarter]
    hid[f] = (gate_act / (1.0 + jnp.exp(-gate_act)) * both[:, quarter:]).astype(bf16)
    hid_c = []
    for x in (3, 2, 1):
        hid_c.append(remote(hid.at[f], hid.at[f], hid_s.at[x], hid_r.at[x], s, peers[x]))
        hid_c[-1].start()

    q_c[1].wait_recv()
    o_c = attend(1)

    o_c += attend(2)
    for c in hid_c:
        c.wait_recv()
    loads[2].wait()
    acc = jnp.zeros((n_seq * CAPACITY, cols), f32)
    for j in range(GROUP):
        acc = acc + jnp.dot(
            hid[j], down_v[j * quarter : (j + 1) * quarter, :], preferred_element_type=f32
        )
    acc = acc.astype(bf16).astype(f32)
    for i in range(n_seq):
        down_out[i] = acc[i * CAPACITY : (i + 1) * CAPACITY, :]
    down_in[s] = down_out[s]
    dn_c = []
    for k in range(1, n_seq):
        to = lax.rem(s + k, n_seq)
        dn_c.append(remote(down_out.at[to], down_in.at[s], dn_s.at[k], dn_r.at[k], to, f))
        dn_c[-1].start()

    q_c[2].wait_recv()
    o_c += attend(3)

    for c in o_c:
        c.wait_recv()
    stat = [st_buf[0]] + [st_in[x] for x in (1, 2, 3)]
    for h in range(heads):
        tops = [v[:, h : h + 1] for v in stat]
        totals = [v[:, heads + h : heads + h + 1] for v in stat]
        top = jnp.maximum(jnp.maximum(tops[0], tops[1]), jnp.maximum(tops[2], tops[3]))
        share = [t * jnp.exp2((m - top) * scale2) for t, m in zip(totals, tops)]
        whole = share[0] + share[1] + share[2] + share[3]
        out = o_own[h] * share[0]
        for x in (1, 2, 3):
            out = out + o_in[x, h].astype(f32) * share[x]
        out = (out / whole).reshape(n_seq, toks, V_DIM).astype(bf16)
        fin[:, :, h * V_DIM : (h + 1) * V_DIM] = out
    hop[f, s] = fin[s]
    fin_c, hop_c = [], []
    for k in range(1, n_seq):
        to = lax.rem(s + k, n_seq)
        fin_c.append(remote(fin.at[to], hop.at[f, s], fin_s.at[k], fin_r.at[k], to, f))
        fin_c[-1].start()
    for c in dn_c:
        c.wait_recv()
    mixed = jnp.zeros((toks, cols), f32)
    for r in range(slots):
        mixed = mixed + mix[:, r : r + 1] * down_in[
            r // CAPACITY, r % CAPACITY : r % CAPACITY + 1, :
        ]
    routed_out[...] = mixed.astype(bf16)

    for c in fin_c:
        c.wait_recv()
    for x in (3, 2, 1):
        hop_c.append(remote(hop.at[f], hop.at[f], hop_s.at[x], hop_r.at[x], s, peers[x]))
        hop_c[-1].start()
    block = heads * V_DIM
    hop_c = [None] + hop_c[::-1]
    for x in range(GROUP):
        if x:
            hop_c[x].wait_recv()
        for r in range(n_seq):
            at = pl.multiple_of((r * GROUP + peers[x]) * block, 128)
            att_out[:, pl.ds(at, block)] = hop[peers[x], r]
    for c in rows_c + proj_c + part_c + q_c + hid_c + dn_c + o_c + fin_c + hop_c[1:]:
        c.wait_send()


def fused(
    n_seq, projected, cached, stream, norm_gain, routes, route_gates, gate_weight, up_weight,
    down_weight,
):
    f32, bf16 = jnp.float32, jnp.bfloat16
    toks = stream.shape[0]
    span = n_seq * toks
    heads = cached.shape[0] // GROUP
    cols = down_weight.shape[1]
    quarter = gate_weight.shape[1] // GROUP
    slots = n_seq * CAPACITY
    vmem = pl.BlockSpec(memory_space=pltpu.VMEM)
    hbm = pl.BlockSpec(memory_space=pl.ANY)
    dma = pltpu.SemaphoreType.DMA
    scratch = [
        pltpu.VMEM((n_seq, toks, heads * (2 * QK_DIM + V_DIM)), bf16),
        pltpu.VMEM((GROUP, heads, span, QK_DIM), bf16),
        pltpu.VMEM((heads, span, QK_DIM), bf16),
        pltpu.VMEM((heads, span, V_DIM), bf16),
        pltpu.VMEM(cached.shape, bf16),
        pltpu.VMEM(gate_weight.shape, bf16),
        pltpu.VMEM(up_weight.shape, bf16),
        pltpu.VMEM(down_weight.shape, bf16),
        pltpu.VMEM((n_seq, CAPACITY, cols), f32),
        pltpu.VMEM((n_seq, CAPACITY, cols), f32),
        pltpu.VMEM((GROUP, slots, 2 * quarter), f32),
        pltpu.VMEM((GROUP, slots, 2 * quarter), f32),
        pltpu.VMEM((GROUP, slots, quarter), bf16),
        pltpu.VMEM((n_seq, CAPACITY, cols), f32),
        pltpu.VMEM((n_seq, CAPACITY, cols), f32),
        pltpu.VMEM((heads, span, V_DIM), f32),
        pltpu.VMEM((GROUP, heads, span, V_DIM), bf16),
        pltpu.VMEM((GROUP, heads, span, V_DIM), bf16),
        pltpu.VMEM((GROUP, span, 128), f32),
        pltpu.VMEM((GROUP, span, 128), f32),
        pltpu.VMEM((n_seq, toks, heads * V_DIM), bf16),
        pltpu.VMEM((GROUP, n_seq, toks, heads * V_DIM), bf16),
        dma((3 + GROUP,)),
        dma,
        dma((n_seq,)), dma((n_seq,)), dma((n_seq,)), dma((n_seq,)),
        dma((GROUP,)), dma((GROUP,)), dma((GROUP,)), dma((GROUP,)),
        dma((GROUP,)), dma((GROUP,)),
        dma((n_seq,)), dma((n_seq,)),
        dma((GROUP,)), dma((GROUP,)), dma((GROUP,)), dma((GROUP,)),
        dma((n_seq,)), dma((n_seq,)), dma((GROUP,)), dma((GROUP,)),
    ]
    return pl.pallas_call(
        functools.partial(one_kernel, n_seq),
        out_shape=(
            jax.ShapeDtypeStruct((toks, cached.shape[0] * n_seq * V_DIM), bf16),
            jax.ShapeDtypeStruct((toks, cols), bf16),
        ),
        in_specs=[hbm, hbm, vmem, vmem, vmem, vmem, hbm, hbm, hbm],
        out_specs=(vmem, vmem),
        scratch_shapes=scratch,
        compiler_params=pltpu.CompilerParams(
            collective_id=0, has_side_effects=True, vmem_limit_bytes=58 * 1024 * 1024
        ),
        cost_estimate=pl.CostEstimate(
            flops=2_000_000_000, bytes_accessed=42_000_000, transcendentals=2_000_000
        ),
    )(
        projected, cached, stream, norm_gain.reshape(1, -1), routes, route_gates,
        gate_weight, up_weight, down_weight,
    )


def fits(mesh, projected, cached):
    n_seq, n_fsdp = mesh.shape["seq"], mesh.shape["fsdp"]
    return (
        n_seq == WAVE_EXPERTS
        and n_fsdp == GROUP
        and projected.shape[0] == 8 * n_seq
        and cached.shape[0] == 16 * n_seq
        and cached.shape[2] == 1792 * n_fsdp
    )


def solution(mesh):
    placed = (
        P("seq", None),
        P("seq", None, "fsdp"),
        P("seq", None),
        P(),
        P("seq", None),
        P("seq", None),
        P("fsdp", "seq"),
        P("fsdp", "seq"),
        P("seq", "fsdp"),
    )
    outs = (P("seq", None), P("seq", "fsdp"))

    def program(projected, cached, *others):
        if fits(mesh, projected, cached):
            body = functools.partial(fused, mesh.shape["seq"])
        else:
            body = on_device
        mapped = jax.shard_map(body, mesh=mesh, in_specs=placed, out_specs=outs, check_vma=False)
        return mapped(projected, cached, *others)

    return program
```
